512 devices in a mesh: section: 16 (over x, y_hi, core), dp: 32 (over z, y_lo).
Axes of the slice: x: 4, y: 8 (y_hi: 2, y_lo: 4; y = y_hi * 4 + y_lo), z: 8, core: 2. Of those that a mesh axis runs over, the one named last changes fastest.
Arguments:
- acts: bfloat16 [16, 4096, 3584], P('section', 'dp'), may hold values from -6 to 6
- norm_gain: float32 [16, 3584], P('section'), may hold values from 0.1 to 1.9
- proj: bfloat16 [16, 3584, 512], P('section', 'dp'), may hold values from -0.25 to 0.25
- out_grad: bfloat16 [16, 4096, 512], P('section', 'dp'), may hold values from -6 to 6
- owner_slot: int32 [16, 7], P('section'), may hold values from 0 to 31, as said below
- left_root: bfloat16 [16, 32, 512, 512], P('section', 'dp'), as said below
- right_root: bfloat16 [16, 32, 512, 512], P('section', 'dp'), as said below
Outputs:
- section_grad: bfloat16 [16, 4096, 3584], P('section', 'dp')
- left_gram: bfloat16 [16, 32, 512, 512], P('section', 'dp')
- right_gram: bfloat16 [16, 32, 512, 512], P('section', 'dp')
- precond: bfloat16 [16, 32, 512, 512], P('section', 'dp')
The draws below stay inside these ranges and needn't reach their ends.
Inputs may be any that keep to these rules, and one draw needn't show every extreme that they name: `owner_slot`: in each layer the 7 values are distinct; place k belongs to index k // 1 of dp; no index of dp receives more than 1 block. `left_root`: Symmetric. `right_root`: Symmetric.
All inputs are finite; a program needn't handle non-finite values.
Results may differ from the reference program's by a relative error of at most 0.034.
Values may be sent and summed in bfloat16 or wider, within the bound.
No kernel may reach another device: no remote copies, remote signals or barrier semaphores. Data moves between devices by JAX's collectives and lax.ppermute only.
A program may use at most 128 MiB of HBM per device.

```python
import jax
import jax.numpy as jnp
from jax import lax

DW = 3584
KW = 512
BS = 512
TOK_DEV = 128
SECTIONS = 16
TOKENS = 4096
NBR = 7
NBC = 1
NBLK = 7
CAP = 1
N_DP = 32


def symmetric(noise, diagonal, off_scale):
    eye = jnp.eye(noise.shape[-1], dtype=jnp.float32)
    off = (noise + jnp.swapaxes(noise, -1, -2)) * off_scale
    return off * (1.0 - eye) + diagonal[..., None] * eye


def draw_owner_slot(key, part):
    key = jax.random.fold_in(key, 5)
    places = N_DP * CAP

    def one_section(section_key):
        key_a, key_b, key_c = jax.random.split(section_key, 3)
        full_owner = jax.random.randint(key_a, (), 0, N_DP)
        others = jax.random.permutation(key_b, places - CAP)[:NBLK - CAP]
        others = jnp.where(others >= full_owner * CAP, others + CAP, others)
        first = full_owner * CAP + jnp.arange(CAP)
        chosen = jnp.concatenate([first, others]).astype(jnp.int32)
        return chosen[jax.random.permutation(key_c, NBLK)]
    return jax.vmap(one_section)(jax.random.split(key, SECTIONS))


def draw_left_root(key, part):
    key = jax.random.fold_in(key, 17)
    key_d, key_o = jax.random.split(key)
    shape = (SECTIONS, N_DP * CAP, BS, BS)
    noise = jax.random.normal(key_o, shape, jnp.float32)
    diagonal = jax.random.uniform(key_d, shape[:-1], jnp.float32, 0.6, 1.4)
    return symmetric(noise, diagonal, 0.03).astype(jnp.bfloat16)


def draw_right_root(key, part):
    key = jax.random.fold_in(key, 19)
    key_d, key_o = jax.random.split(key)
    shape = (SECTIONS, N_DP * CAP, BS, BS)
    noise = jax.random.normal(key_o, shape, jnp.float32)
    diagonal = jax.random.uniform(key_d, shape[:-1], jnp.float32, 0.6, 1.4)
    return symmetric(noise, diagonal, 0.03).astype(jnp.bfloat16)


def levels(rng, dims, pieces, least, largest):
    factor_of, own = 1.0, jax.random.fold_in(rng, 6)
    for position, parts in pieces:
        steps = jnp.exp(jax.random.uniform(jax.random.fold_in(own, position), (parts,), jnp.float32, least / len(pieces), largest / len(pieces)))
        factor_of = factor_of * jnp.repeat(steps, dims[position] // parts).reshape([-1 if axis == position else 1 for axis in range(len(dims))])
    return factor_of


def scatter_about(key, dims, spread, limit, cuts=(), kind=jnp.bfloat16):
    level = levels(key, dims, cuts, -0.22, 0.18) if cuts else 1.0
    values = jax.random.normal(key, dims, jnp.float32) * spread * level
    return jnp.minimum(jnp.maximum(values, -limit), limit).astype(kind)


def setup_inputs(seed: int = 0) -> dict:
    splits = jax.random.split(jax.random.key(seed), 8)
    return {
        "acts": scatter_about(splits[0], (SECTIONS, TOKENS, DW), 1.0, 6.0, ((0, 16), (1, 32))),
        "norm_gain": jnp.clip(1.0 + 0.18 * jax.random.normal(splits[1], (SECTIONS, DW), jnp.float32), 0.1, 1.9),
        "proj": scatter_about(splits[2], (SECTIONS, DW, KW), KW ** -0.5, 0.25, ((0, 16), (1, 32))),
        "out_grad": scatter_about(splits[3], (SECTIONS, TOKENS, KW), 1.0, 6.0, ((0, 16), (1, 32))),
        "owner_slot": draw_owner_slot(jax.random.fold_in(splits[7], 71), 0),
        "left_root": draw_left_root(jax.random.fold_in(splits[7], 71), 0),
        "right_root": draw_right_root(jax.random.fold_in(splits[7], 71), 0),
    }


norm_eps = 1e-06

def reference(acts, norm_gain, proj, out_grad, owner_slot, left_root, right_root):
    scale = TOKENS ** (-0.5)
    places = N_DP * CAP
    running = jnp.zeros((TOKENS, DW), jnp.float32)
    section_out = [None] * SECTIONS
    lefts = []
    rights = []
    preconds = []
    for section in range(SECTIONS - 1, -1, -1):
        stream = acts[section].astype(jnp.float32)
        gain = norm_gain[section].astype(jnp.float32)
        radius = jnp.sqrt(lax.optimization_barrier(jnp.mean(stream * stream, axis=1, keepdims=True)) + norm_eps)
        unit = stream / radius
        normed = (unit * gain).astype(jnp.bfloat16)
        back = jnp.dot(out_grad[section], proj[section].T, preferred_element_type=jnp.float32)
        scaled = back * gain
        inner = lax.optimization_barrier(jnp.mean(scaled * unit, axis=1, keepdims=True))
        branch = (scaled - unit * inner) / radius
        running = running + branch
        section_out[section] = running.astype(jnp.bfloat16)
        normed_parts = normed.reshape(N_DP, TOK_DEV, DW)
        upstream_parts = out_grad[section].reshape(N_DP, TOK_DEV, KW)

        def add_part(total, pair):
            normed_part, upstream_part = pair
            term = jnp.dot(normed_part.T, upstream_part, preferred_element_type=jnp.float32) * scale
            term = lax.optimization_barrier(term.astype(jnp.bfloat16)).astype(jnp.float32)
            return (total + term, None)
        summed, _ = lax.scan(add_part, jnp.zeros((DW, KW), jnp.float32), (normed_parts, upstream_parts))
        grad = summed.astype(jnp.bfloat16).astype(jnp.float32)
        tiles = grad.reshape(NBR, BS, NBC, BS).transpose(0, 2, 1, 3).reshape(NBLK, BS, BS)
        selector = (owner_slot[section][None, :] == jnp.arange(places, dtype=jnp.int32)[:, None]).astype(jnp.float32)
        grads = jnp.einsum('sm,mij->sij', selector, tiles).astype(jnp.bfloat16).astype(jnp.float32)
        gram_left = jnp.einsum('sij,skj->sik', grads, grads) / BS
        gram_right = jnp.einsum('sji,sjk->sik', grads, grads) / BS
        lefts.append(gram_left.astype(jnp.bfloat16))
        rights.append(gram_right.astype(jnp.bfloat16))
        middle = jnp.einsum('sij,sjk->sik', left_root[section].astype(jnp.float32), grads).astype(jnp.bfloat16)
        preconds.append(jnp.einsum('sij,sjk->sik', middle.astype(jnp.float32), right_root[section].astype(jnp.float32)).astype(jnp.bfloat16))
    section_grad = jnp.stack(section_out)
    left_gram = jnp.stack(lefts[::-1])
    right_gram = jnp.stack(rights[::-1])
    precond = jnp.stack(preconds[::-1])
    return (section_grad, left_gram, right_gram, precond)
```

```python
import jax
import jax.numpy as jnp
from jax import lax
from jax.sharding import Mesh, PartitionSpec as P

norm_eps = 1e-06
SEC = ("x", "yh", "c")
DP = ("z", "yl")
PAIRS = ("x", "yh")
NX, NYH, NC, NZ, NYL = 4, 2, 2, 8, 4
NPAIR = NX * NYH


def swap_cores(value):
    return lax.ppermute(value, "c", [(0, 1), (1, 0)])


def shift_z(value, by):
    return lax.ppermute(value, "z", [(i, (i + by) % NZ) for i in range(NZ)])


def gather_rows(shard):
    rows, width = shard.shape
    copies = jnp.broadcast_to(shard[None], (NYL, rows, width))
    mine = lax.all_to_all(copies, "yl", 0, 0).reshape(NYL * rows, width)
    block = NYL * rows
    half = block // 2
    z = lax.axis_index("z")
    up = down = mine
    parts = [(mine, 0, 0)]
    for step in range(1, NZ // 2):
        up = shift_z(up, 1)
        down = shift_z(down, -1)
        parts += [(up, -step, 0), (down, step, 0)]
    parts += [(shift_z(up[:half], 1), NZ // 2, 0), (shift_z(down[half:], -1), NZ // 2, half)]
    full = jnp.zeros((NZ * block, width), shard.dtype)
    for value, offset, low in parts:
        place = lax.rem(z + offset + NZ, NZ) * block + low
        full = lax.dynamic_update_slice(full, value, (place, 0))
    return full


def later_sections(branch):
    tokens, width = branch.shape
    half = tokens // 2
    core = lax.axis_index("c")
    last = core == 1
    rounded = branch.astype(jnp.bfloat16)
    own_half = jnp.where(last, branch[half:], branch[:half])
    away = jnp.where(last, rounded[:half], rounded[half:])
    other = swap_cores(away).astype(jnp.float32)
    total = (own_half + other).astype(jnp.bfloat16)
    spread = lax.all_to_all(total.reshape(NPAIR, half // NPAIR, width), PAIRS, 0, 0)
    run = jnp.zeros(spread.shape[1:], jnp.float32)
    sums = [None] * NPAIR
    for pair in range(NPAIR - 1, -1, -1):
        sums[pair] = run.astype(jnp.bfloat16)
        run = run + spread[pair].astype(jnp.float32)
    after = lax.all_to_all(jnp.stack(sums), PAIRS, 0, 0).reshape(half, width)
    after = after.astype(jnp.float32)
    give = after + jnp.where(last, own_half, 0.0)
    take = swap_cores(give.astype(jnp.bfloat16)).astype(jnp.float32)
    kept = own_half + after + jnp.where(last, 0.0, other)
    low = jnp.where(last, branch[:half] + take, kept)
    high = jnp.where(last, kept, branch[half:] + take)
    return jnp.concatenate([low, high]).astype(jnp.bfloat16)


def grad_shard(acts, shared, gain, scale):
    tokens, width = acts.shape
    keys = shared.shape[1]
    block = 512
    count = width // block
    part = block // NYL
    piece = part // NZ
    j = lax.axis_index("yl")
    z = lax.axis_index("z")
    quarters = acts.reshape(tokens, count, NYL, part).transpose(2, 0, 1, 3).reshape(NYL, tokens, count * part)
    rows = []
    for k in range(NYL):
        mine = lax.dynamic_index_in_dim(quarters, j ^ k, 0, False)
        load = jnp.concatenate([mine, shared], axis=1)
        if k:
            load = lax.ppermute(load, "yl", [(i, i ^ k) for i in range(NYL)])
        rows.append(load)
    rows = jnp.concatenate(rows)
    partial = lax.dot_general(
        rows[:, : count * part], rows[:, count * part :], (((0,), (0,)), ((), ())), preferred_element_type=jnp.float32
    )
    partial = partial.astype(jnp.bfloat16).reshape(count, NZ, piece, keys).transpose(1, 0, 2, 3)
    total = 0.0
    for k in range(NZ):
        term = lax.dynamic_index_in_dim(partial, lax.rem(z + k, NZ), 0, False)
        if k:
            term = shift_z(term, k)
        total = total + term.astype(jnp.float32)
    gains = gain.reshape(count, NYL, NZ, piece)
    gains = lax.dynamic_index_in_dim(gains, j, 1, False)
    gains = lax.dynamic_index_in_dim(gains, z, 1, False)
    return (total * (gains * scale)[:, :, None]).astype(jnp.bfloat16)


def to_owner(shard, owners):
    count, piece, keys = shard.shape
    places = jnp.arange(NZ * NYL, dtype=jnp.int32)
    match = (owners[None, :] == places[:, None]).astype(jnp.bfloat16)
    send = jnp.einsum("pb,brk->prk", match, shard, preferred_element_type=jnp.float32).astype(jnp.bfloat16)
    got = lax.all_to_all(send, DP, 0, 0)
    return got.reshape(NZ, NYL, piece, keys).transpose(1, 0, 2, 3).reshape(NZ * NYL * piece, keys)


def body(acts, norm_gain, proj, out_grad, owner_slot, left_root, right_root):
    acts, gain, upstream = acts[0], norm_gain[0], out_grad[0]
    tokens = acts.shape[0] * NZ * NYL
    stream = acts.astype(jnp.float32)
    radius = jnp.sqrt(jnp.mean(stream * stream, axis=1, keepdims=True) + norm_eps)
    weights = gather_rows(proj[0])
    shared = (upstream.astype(jnp.float32) / radius).astype(jnp.bfloat16)
    shard = grad_shard(acts, shared, gain, tokens ** (-0.5))

    back = lax.dot_general(upstream, weights, (((1,), (1,)), ((), ())), preferred_element_type=jnp.float32)
    unit = stream / radius
    scaled = back * gain
    inner = jnp.mean(scaled * unit, axis=1, keepdims=True)
    branch = (scaled - unit * inner) / radius
    section_grad = later_sections(branch)[None]

    grads = to_owner(shard, owner_slot[0])
    block = grads.shape[0]

    def dot(a, b, dims):
        return lax.dot_general(a, b, (dims, ((), ())), preferred_element_type=jnp.float32)

    left_gram = (dot(grads, grads, ((1,), (1,))) / block).astype(jnp.bfloat16)
    right_gram = (dot(grads, grads, ((0,), (0,))) / block).astype(jnp.bfloat16)
    middle = dot(left_root[0, 0], grads, ((1,), (0,))).astype(jnp.bfloat16)
    precond = dot(middle, right_root[0, 0], ((1,), (0,))).astype(jnp.bfloat16)
    return section_grad, left_gram[None, None], right_gram[None, None], precond[None, None]


def solution(mesh):
    split = Mesh(mesh.devices.reshape(NX, NYH, NC, NZ, NYL), (*SEC, *DP))
    in_specs = (
        P(SEC, DP, None),
        P(SEC, None),
        P(SEC, DP, None),
        P(SEC, DP, None),
        P(SEC, None),
        P(SEC, DP, None, None),
        P(SEC, DP, None, None),
    )
    out_specs = (
        P(SEC, DP, None),
        P(SEC, DP, None, None),
        P(SEC, DP, None, None),
        P(SEC, DP, None, None),
    )
    return jax.shard_map(body, mesh=split, in_specs=in_specs, out_specs=out_specs, check_vma=False)
```

```python
import jax
import jax.numpy as jnp
from jax import lax
from jax.experimental import pallas as pl
from jax.experimental.pallas import tpu as pltpu
from jax.sharding import Mesh, PartitionSpec as P

norm_eps = 1e-06
SEC = ("x", "yh", "c")
DP = ("z", "yl")
NX, NYH, NC, NZ, NYL = 4, 2, 2, 8, 4
NSEC = NX * NYH * NC
LANES = 128
GROUP = 16
BF16, F32 = jnp.bfloat16, jnp.float32


def call(kernel, outs, args, scratch=(), flops=0, smem=()):
    specs = [pl.BlockSpec(memory_space=pltpu.SMEM if i in smem else pltpu.VMEM) for i in range(len(args))]
    moved = sum(a.size * a.dtype.itemsize for a in (*args, *outs))
    return pl.pallas_call(
        kernel,
        out_shape=outs,
        in_specs=specs,
        out_specs=[pl.BlockSpec(memory_space=pltpu.VMEM) for _ in outs],
        scratch_shapes=list(scratch),
        compiler_params=pltpu.CompilerParams(vmem_limit_bytes=16 * 2**20),
        cost_estimate=pl.CostEstimate(flops=flops, bytes_accessed=moved, transcendentals=0),
    )(*args)


def shape(*dims, dtype=BF16):
    return jax.ShapeDtypeStruct(dims, dtype)


def shift_z(value, by):
    return lax.ppermute(value, "z", [(i, (i + by) % NZ) for i in range(NZ)])


def swap_y(value, k):
    return lax.ppermute(value, "yl", [(i, i ^ k) for i in range(NYL)])


def dot(a, b, dims):
    return lax.dot_general(a, b, (dims, ((), ())), preferred_element_type=F32)


def tie(*values):
    return lax.optimization_barrier(values)


def prepare_kernel(acts, upstream, send, turned):
    tokens, width = acts.shape
    keys = upstream.shape[1]
    rows = width // (NZ * NYL)
    stream = acts[...].astype(F32)
    radius = jnp.sqrt(jnp.mean(stream * stream, axis=1, keepdims=True) + norm_eps)
    for i in range(width // LANES):
        at = slice(i * LANES, (i + 1) * LANES)
        turned[at, :] = acts[:, at].astype(F32).T.astype(BF16)
    for j in range(NYL):
        for z in range(NZ):
            low = (z * NYL + j) * rows
            send[j, z * rows : (z + 1) * rows, :] = turned[low : low + rows, :]
    for i in range(keys // LANES):
        at = slice(i * LANES, (i + 1) * LANES)
        shared = (upstream[:, at].astype(F32) / radius).T.astype(BF16)
        low = NZ * rows + i * LANES
        for j in range(NYL):
            send[j, low : low + LANES, :] = shared


def product_kernel(scale, got, weights, gains, scaled, stats, tile, *rest):
    chunks, shared, held = rest
    tokens = got.shape[2]
    width = weights.shape[0]
    rows = width // NZ
    for t in range(NYL):
        at = slice(t * tokens, (t + 1) * tokens)
        tile[:, at] = got[t, :width, :]
        shared[:, at] = got[t, width:, :]
    up = shared[...]
    cross = jnp.zeros((1, NYL * tokens), F32)
    square = jnp.zeros((1, NYL * tokens), F32)
    for z in range(NZ):
        at = slice(z * rows, (z + 1) * rows)
        here = tile[at, :]
        value = dot(weights[at, :], up, ((1,), (0,))) * gains[at, :]
        scaled[at, :] = value
        wide = here.astype(F32)
        cross = cross + jnp.sum(value * wide, axis=0, keepdims=True)
        square = square + jnp.sum(wide * wide, axis=0, keepdims=True)
        held[at, :] = (dot(here, up, ((1,), (1,))) * (gains[at, :] * scale)).astype(BF16)
    stats[0:1, :] = cross
    stats[1:2, :] = square
    j = lax.axis_index("yl")
    for k in range(NZ):
        for i in range(rows // GROUP):
            z = lax.rem(lax.div(7 * j + i, 4) - k + NZ, NZ)
            chunks[k, i] = held[pl.ds(pl.multiple_of(z * rows + i * GROUP, GROUP), GROUP), :]


def branch_kernel(full, scaled, tile, stats, out):
    pull = stats[0:1, :] / full / (stats[1:2, :] / full + norm_eps)
    width = scaled.shape[0]
    rows = width // NZ
    half = rows // 2
    for z in range(NZ):
        at = slice(z * rows, (z + 1) * rows)
        value = scaled[at, :] - tile[at, :].astype(F32) * pull
        out[2 * z] = value[:half].astype(BF16)
        out[2 * z + 1] = value[half:].astype(BF16)


def suffix_kernel(spread, out):
    run = jnp.zeros(spread.shape[1:], F32)
    for section in range(NSEC - 1, -1, -1):
        run = run + spread[section].astype(F32)
        for t in range(NYL):
            out[section * NYL + t] = run[:, t * LANES : (t + 1) * LANES].astype(BF16)


def final_kernel(got, out, turned):
    half = got.shape[1]
    for i in range(NSEC):
        for j in range(NYL):
            low = ((i // 2) * NYL + j) * 2 * half + (i % 2) * half
            turned[low : low + half, :] = got[i * NYL + j].astype(F32)
    for i in range(out.shape[1] // LANES):
        at = slice(i * LANES, (i + 1) * LANES)
        out[:, at] = turned[at, :].T.astype(BF16)


def sum_kernel(terms, out):
    total = terms[0].astype(F32)
    for k in range(1, NZ):
        total = total + terms[k].astype(F32)
    out[...] = total.astype(BF16)


def route_kernel(owners, *refs):
    parts, outs, stage = refs[:NYL], refs[NYL:-1], refs[-1]
    for k, part in enumerate(parts):
        stage[k] = part[...]
    z = lax.axis_index("z")
    j = lax.axis_index("yl")
    per = parts[0].shape[0]
    for k, out in enumerate(outs):
        out[...] = jnp.zeros_like(out)
        place = lax.rem(z + k, NZ) * NYL + j
        for b in range(owners.shape[1]):

            @pl.when(owners[0, b] == place)
            def _():
                for q in range(NYL):
                    group = 32 * b + NYL * z + q
                    shard = lax.div(group, per)
                    which = lax.rem(shard, NYL) ^ j
                    out[q * GROUP : (q + 1) * GROUP, :] = stage[which, group - shard * per]


def shampoo_kernel(*refs):
    *parts, left, right, left_gram, right_gram, precond, grads = refs
    z = lax.axis_index("z")
    rows = parts[0].shape[0]
    for k, part in enumerate(parts):
        grads[pl.ds(pl.multiple_of(lax.rem(z + NZ - k, NZ) * rows, rows), rows), :] = part[...]
    block = grads[...]
    middle = dot(left[...], block, ((1,), (0,))).astype(BF16)
    precond[...] = dot(middle, right[...], ((1,), (0,))).astype(BF16)
    left_gram[...] = (dot(block, block, ((1,), (1,))) / block.shape[0]).astype(BF16)
    right_gram[...] = (dot(block, block, ((0,), (0,))) / block.shape[0]).astype(BF16)


def body(acts, norm_gain, proj, out_grad, owner_slot, left_root, right_root):
    acts, gain, upstream, shard = acts[0], norm_gain[0], out_grad[0], proj[0]
    tokens, width = acts.shape
    rows, keys = shard.shape
    side = left_root.shape[-1]
    quarter = width // NYL
    line = NYL * tokens
    per = rows // GROUP

    (send,) = call(
        prepare_kernel,
        [shape(NYL, quarter + keys, tokens)],
        [acts, upstream],
        scratch=[pltpu.VMEM((width, tokens), BF16)],
    )
    got = lax.all_to_all(send, "yl", 0, 0)
    gains = lax.dynamic_index_in_dim(gain.reshape(NZ, NYL, rows), lax.axis_index("yl"), 1, False)
    gains = gains.reshape(quarter, 1)
    weights = lax.all_gather(shard, "z", axis=0, tiled=True)
    got, weights, gains = tie(got, weights, gains)
    scale = (tokens * NZ * NYL) ** (-0.5)
    scaled, stats, tile, chunks = call(
        lambda *refs: product_kernel(scale, *refs),
        [
            shape(quarter, line, dtype=F32),
            shape(2, line, dtype=F32),
            shape(quarter, line),
            shape(NZ, per, GROUP, keys),
        ],
        [got, weights, gains],
        scratch=[pltpu.VMEM((keys, line), BF16), pltpu.VMEM((quarter, keys), BF16)],
        flops=4 * quarter * line * keys,
    )
    terms = lax.all_to_all(chunks, "z", 0, 0)
    stats = lax.psum(stats, "yl")
    (branch,) = call(
        lambda *refs: branch_kernel(width, *refs),
        [shape(NSEC, quarter // NSEC, line)],
        [scaled, tile, stats],
    )
    branch, terms = tie(branch, terms)
    spread = lax.all_to_all(branch, SEC, 0, 0)

    (grads,) = call(sum_kernel, [shape(per, GROUP, keys)], [terms])
    parts = [grads] + [swap_y(grads, k) for k in range(1, NYL)]
    spread, *parts = tie(spread, *parts)
    (sums,) = call(suffix_kernel, [shape(NSEC * NYL, quarter // NSEC, tokens)], [spread])
    home = lax.all_to_all(sums, (*SEC, "yl"), 0, 0)
    parts = call(
        route_kernel,
        [shape(side // NZ, keys)] * NZ,
        [owner_slot, *parts],
        scratch=[pltpu.VMEM((NYL, per, GROUP, keys), BF16)],
        smem=(0,),
    )
    parts = [parts[0]] + [shift_z(parts[k], k) for k in range(1, NZ)]
    home, *parts = tie(home, *parts)
    (section_grad,) = call(
        final_kernel, [shape(tokens, width)], [home], scratch=[pltpu.VMEM((width, tokens), F32)]
    )
    out = shape(side, side)
    left_gram, right_gram, precond = call(
        shampoo_kernel,
        [out, out, out],
        [*parts, left_root[0, 0], right_root[0, 0]],
        scratch=[pltpu.VMEM((side, side), BF16)],
        flops=8 * side**3,
    )
    return section_grad[None], left_gram[None, None], right_gram[None, None], precond[None, None]


def solution(mesh):
    split = Mesh(mesh.devices.reshape(NX, NYH, NC, NZ, NYL), (*SEC, *DP))
    in_specs = (
        P(SEC, DP, None),
        P(SEC, None),
        P(SEC, DP, None),
        P(SEC, DP, None),
        P(SEC, None),
        P(SEC, DP, None, None),
        P(SEC, DP, None, None),
    )
    out_specs = (
        P(SEC, DP, None),
        P(SEC, DP, None, None),
        P(SEC, DP, None, None),
        P(SEC, DP, None, None),
    )
    return jax.shard_map(body, mesh=split, in_specs=in_specs, out_specs=out_specs, check_vma=False)
```

```python
import jax
import jax.numpy as jnp
from jax import lax
from jax.experimental import pallas as pl
from jax.experimental.pallas import tpu as pltpu
from jax.sharding import Mesh, PartitionSpec as P

norm_eps = 1e-06
SEC = ("x", "yh", "c")
DP = ("z", "yl")
NX, NYH, NC, NZ, NYL = 4, 2, 2, 8, 4
PAIRS = ("x", "yh")
NPAIR = NX * NYH
LANES = 128
GROUP = 16
BF16, F32 = jnp.bfloat16, jnp.float32


def call(kernel, outs, args, scratch=(), flops=0, smem=()):
    specs = [pl.BlockSpec(memory_space=pltpu.SMEM if i in smem else pltpu.VMEM) for i in range(len(args))]
    moved = sum(a.size * a.dtype.itemsize for a in (*args, *outs))
    return pl.pallas_call(
        kernel,
        out_shape=outs,
        in_specs=specs,
        out_specs=[pl.BlockSpec(memory_space=pltpu.VMEM) for _ in outs],
        scratch_shapes=list(scratch),
        compiler_params=pltpu.CompilerParams(vmem_limit_bytes=16 * 2**20),
        cost_estimate=pl.CostEstimate(flops=flops, bytes_accessed=moved, transcendentals=0),
    )(*args)


def shape(*dims, dtype=BF16):
    return jax.ShapeDtypeStruct(dims, dtype)


def shift_z(value, by):
    return lax.ppermute(value, "z", [(i, (i + by) % NZ) for i in range(NZ)])


def swap_cores(value):
    return lax.ppermute(value, "c", [(0, 1), (1, 0)])


def swap_y(value, k):
    return lax.ppermute(value, "yl", [(i, i ^ k) for i in range(NYL)])


def dot(a, b, dims):
    return lax.dot_general(a, b, (dims, ((), ())), preferred_element_type=F32)


def tie(*values):
    return lax.optimization_barrier(values)


def prepare_kernel(acts, upstream, send, turned):
    tokens, width = acts.shape
    keys = upstream.shape[1]
    rows = width // (NZ * NYL)
    stream = acts[...].astype(F32)
    radius = jnp.sqrt(jnp.mean(stream * stream, axis=1, keepdims=True) + norm_eps)
    for i in range(width // LANES):
        at = slice(i * LANES, (i + 1) * LANES)
        turned[at, :] = acts[:, at].astype(F32).T.astype(BF16)
    for j in range(NYL):
        for z in range(NZ):
            low = (z * NYL + j) * rows
            send[j, z * rows : (z + 1) * rows, :] = turned[low : low + rows, :]
    for i in range(keys // LANES):
        at = slice(i * LANES, (i + 1) * LANES)
        shared = (upstream[:, at].astype(F32) / radius).T.astype(BF16)
        low = NZ * rows + i * LANES
        for j in range(NYL):
            send[j, low : low + LANES, :] = shared


def gradient_kernel(scale, got, gains, keep, give, tile, shared, held):
    tokens = got.shape[2]
    width = gains.shape[0]
    rows = width // NZ
    for t in range(NYL):
        at = slice(t * tokens, (t + 1) * tokens)
        tile[:, at] = got[t, :width, :]
        shared[:, at] = got[t, width:, :]
    up = shared[...]
    for z in range(NZ):
        at = slice(z * rows, (z + 1) * rows)
        held[at, :] = (dot(tile[at, :], up, ((1,), (1,))) * (gains[at, :] * scale)).astype(BF16)
    j = lax.axis_index("yl")
    mine = lax.axis_index("z")
    for k in range(NZ):
        out = give if k % 2 else keep
        to = k - k % 2 + lax.rem(mine + k, 2)
        for i in range(rows // GROUP):
            z = lax.rem(lax.div(7 * j + i, 4) - to + NZ, NZ)
            out[k // 2, i] = held[pl.ds(pl.multiple_of(z * rows + i * GROUP, GROUP), GROUP), :]


def back_kernel(got, weights, gains, scaled, stats, shared):
    tokens = got.shape[2]
    width = weights.shape[0]
    rows = width // NZ
    for t in range(NYL):
        shared[:, t * tokens : (t + 1) * tokens] = got[t, width:, :]
    up = shared[...]
    cross = [jnp.zeros((1, tokens), F32) for _ in range(NYL)]
    square = [jnp.zeros((1, tokens), F32) for _ in range(NYL)]
    for z in range(NZ):
        at = slice(z * rows, (z + 1) * rows)
        value = dot(weights[at, :], up, ((1,), (0,))) * gains[at, :]
        scaled[at, :] = value
        for t in range(NYL):
            wide = got[t, at, :].astype(F32)
            cross[t] = cross[t] + jnp.sum(value[:, t * tokens : (t + 1) * tokens] * wide, axis=0, keepdims=True)
            square[t] = square[t] + jnp.sum(wide * wide, axis=0, keepdims=True)
    for t in range(NYL):
        stats[0:1, t * tokens : (t + 1) * tokens] = cross[t]
        stats[1:2, t * tokens : (t + 1) * tokens] = square[t]


def branch_kernel(full, scaled, got, stats, out):
    pull = stats[0:1, :] / full / (stats[1:2, :] / full + norm_eps)
    tokens = got.shape[2]
    rows = out.shape[1]
    for i in range(NPAIR):
        at = slice(i * rows, (i + 1) * rows)
        for t in range(NYL):
            to = slice(t * tokens, (t + 1) * tokens)
            out[i, :, to] = (scaled[at, to] - got[t, at, :].astype(F32) * pull[:, to]).astype(BF16)


def suffix_kernel(spread, out):
    last = (lax.axis_index("c") == 1).astype(F32)
    run = jnp.zeros(spread.shape[1:], F32)
    for pair in range(NPAIR - 1, -1, -1):
        value = spread[pair].astype(F32)
        out[pair] = (run + value * last).astype(BF16)
        run = run + value


def section_kernel(spread, got, out):
    run = jnp.zeros(spread.shape[1:], F32)
    for pair in range(NPAIR - 1, -1, -1):
        run = run + spread[pair].astype(F32)
        value = run + got[pair].astype(F32)
        for t in range(NYL):
            out[pair * NYL + t] = value[:, t * LANES : (t + 1) * LANES].astype(BF16)


def final_kernel(turned, out):
    for i in range(out.shape[1] // LANES):
        at = slice(i * LANES, (i + 1) * LANES)
        out[:, at] = turned[at, :].astype(F32).T.astype(BF16)


def add_kernel(keep, got, *outs):
    h = lax.div(lax.axis_index("z"), 2)
    for k, out in enumerate(outs):
        at = lax.rem(h + k, NZ // 2)
        out[...] = (keep[at].astype(F32) + got[at].astype(F32)).astype(BF16)


def sum_kernel(*refs):
    *terms, out = refs
    total = terms[0][...].astype(F32)
    for term in terms[1:]:
        total = total + term[...].astype(F32)
    out[...] = total.astype(BF16)


def route_kernel(owners, *refs):
    parts, (keep, give, stage) = refs[:NYL], refs[NYL:]
    for k, part in enumerate(parts):
        stage[k] = part[...]
    z = lax.axis_index("z")
    j = lax.axis_index("yl")
    per = parts[0].shape[0]
    for i in range(NZ):
        out = give if i % 2 else keep
        out[i // 2] = jnp.zeros(out.shape[1:], BF16)
        place = (i - i % 2 + lax.rem(z + i, 2)) * NYL + j
        for b in range(owners.shape[1]):

            @pl.when(owners[0, b] == place)
            def _():
                for q in range(NYL):
                    group = 32 * b + NYL * z + q
                    shard = lax.div(group, per)
                    which = lax.rem(shard, NYL) ^ j
                    out[i // 2, q * GROUP : (q + 1) * GROUP, :] = stage[which, group - shard * per]


def pair_kernel(keep, got, *outs):
    h = lax.div(lax.axis_index("z"), 2)
    for k, out in enumerate(outs):
        at = lax.rem(h + k, NZ // 2)
        out[0] = keep[at]
        out[1] = got[at]


def shampoo_kernel(*refs):
    *parts, left, right, left_gram, right_gram, precond, grads = refs
    z = lax.axis_index("z")
    rows = parts[0].shape[1]
    for k, part in enumerate(parts):
        source = lax.rem(z + NZ - 2 * k, NZ)
        grads[pl.ds(pl.multiple_of(source * rows, rows), rows), :] = part[0]
        grads[pl.ds(pl.multiple_of((source ^ 1) * rows, rows), rows), :] = part[1]
    block = grads[...]
    middle = dot(left[...], block, ((1,), (0,))).astype(BF16)
    precond[...] = dot(middle, right[...], ((1,), (0,))).astype(BF16)
    left_gram[...] = (dot(block, block, ((1,), (1,))) / block.shape[0]).astype(BF16)
    right_gram[...] = (dot(block, block, ((0,), (0,))) / block.shape[0]).astype(BF16)


def body(acts, norm_gain, proj, out_grad, owner_slot, left_root, right_root):
    acts, gain, upstream, shard = acts[0], norm_gain[0], out_grad[0], proj[0]
    tokens, width = acts.shape
    rows, keys = shard.shape
    side = left_root.shape[-1]
    quarter = width // NYL
    line = NYL * tokens
    per = rows // GROUP

    (send,) = call(
        prepare_kernel,
        [shape(NYL, quarter + keys, tokens)],
        [acts, upstream],
        scratch=[pltpu.VMEM((width, tokens), BF16)],
    )
    got = lax.all_to_all(send, "yl", 0, 0)
    gains = lax.dynamic_index_in_dim(gain.reshape(NZ, NYL, rows), lax.axis_index("yl"), 1, False)
    gains = gains.reshape(quarter, 1)
    weights = lax.all_gather(shard, "z", axis=0, tiled=True)
    got, weights, gains = tie(got, weights, gains)
    scale = (tokens * NZ * NYL) ** (-0.5)
    chunk = shape(NZ // 2, per, GROUP, keys)
    chunks, away = call(
        lambda *refs: gradient_kernel(scale, *refs),
        [chunk, chunk],
        [got, gains],
        scratch=[pltpu.VMEM((quarter, line), BF16), pltpu.VMEM((keys, line), BF16), pltpu.VMEM((quarter, keys), BF16)],
        flops=2 * quarter * line * keys,
    )

    near = lax.ppermute(away, "z", [(i, i ^ 1) for i in range(NZ)])
    scaled, stats = call(
        back_kernel,
        [shape(quarter, line, dtype=F32), shape(2, line, dtype=F32)],
        [got, weights, gains],
        scratch=[pltpu.VMEM((keys, line), BF16)],
        flops=2 * quarter * line * keys,
    )
    stats = lax.psum(stats, "yl")
    (branch,) = call(
        lambda *refs: branch_kernel(width, *refs),
        [shape(NPAIR, quarter // NPAIR, line)],
        [scaled, got, stats],
    )
    branch, near = tie(branch, near)

    spread = lax.all_to_all(branch, PAIRS, 0, 0)
    terms = call(add_kernel, [shape(per, GROUP, keys)] * (NZ // 2), [chunks, near])
    terms = [terms[0]] + [shift_z(terms[k], 2 * k) for k in range(1, NZ // 2)]
    (grads,) = call(sum_kernel, [shape(per, GROUP, keys)], terms)
    spread, grads = tie(spread, grads)
    (give,) = call(suffix_kernel, [shape(NPAIR, quarter // NPAIR, line)], [spread])
    take = swap_cores(give)
    parts = [grads] + [swap_y(grads, k) for k in range(1, NYL)]
    (sums,) = call(section_kernel, [shape(NPAIR * NYL, quarter // NPAIR, tokens)], [spread, take])
    sums, *parts = tie(sums, *parts)
    home = lax.all_to_all(sums, (*PAIRS, "yl"), 0, 0).reshape(width, tokens)

    half = shape(NZ // 2, side // NZ, keys)
    keep, away = call(
        route_kernel,
        [half, half],
        [owner_slot, *parts],
        scratch=[pltpu.VMEM((NYL, per, GROUP, keys), BF16)],
        smem=(0,),
    )
    near = lax.ppermute(away, "z", [(i, i ^ 1) for i in range(NZ)])
    parts = call(pair_kernel, [shape(2, side // NZ, keys)] * (NZ // 2), [keep, near])
    parts = [parts[0]] + [shift_z(parts[k], 2 * k) for k in range(1, NZ // 2)]
    out = shape(side, side)
    left_gram, right_gram, precond = call(
        shampoo_kernel,
        [out, out, out],
        [*parts, left_root[0, 0], right_root[0, 0]],
        scratch=[pltpu.VMEM((side, side), BF16)],
        flops=8 * side**3,
    )
    home, left_gram, right_gram, precond = tie(home, left_gram, right_gram, precond)
    (section_grad,) = call(final_kernel, [shape(tokens, width)], [home])
    return section_grad[None], left_gram[None, None], right_gram[None, None], precond[None, None]


def solution(mesh):
    split = Mesh(mesh.devices.reshape(NX, NYH, NC, NZ, NYL), (*SEC, *DP))
    in_specs = (
        P(SEC, DP, None),
        P(SEC, None),
        P(SEC, DP, None),
        P(SEC, DP, None),
        P(SEC, None),
        P(SEC, DP, None, None),
        P(SEC, DP, None, None),
    )
    out_specs = (
        P(SEC, DP, None),
        P(SEC, DP, None, None),
        P(SEC, DP, None, None),
        P(SEC, DP, None, None),
    )
    return jax.shard_map(body, mesh=split, in_specs=in_specs, out_specs=out_specs, check_vma=False)
```

```python
import jax
import jax.numpy as jnp
from jax import lax
from jax.experimental import pallas as pl
from jax.experimental.pallas import tpu as pltpu
from jax.sharding import Mesh, PartitionSpec as P

norm_eps = 1e-06
SEC = ("x", "yh", "c")
DP = ("z", "yl")
NX, NYH, NC, NZ, NYL = 4, 2, 2, 8, 4
PAIRS = ("x", "yh")
NPAIR = NX * NYH
LANES = 128
GROUP = 16
BF16, F32 = jnp.bfloat16, jnp.float32


def call(kernel, outs, args, scratch=(), flops=0, smem=()):
    specs = [pl.BlockSpec(memory_space=pltpu.SMEM if i in smem else pltpu.VMEM) for i in range(len(args))]
    moved = sum(a.size * a.dtype.itemsize for a in (*args, *outs))
    return pl.pallas_call(
        kernel,
        out_shape=outs,
        in_specs=specs,
        out_specs=[pl.BlockSpec(memory_space=pltpu.VMEM) for _ in outs],
        scratch_shapes=list(scratch),
        compiler_params=pltpu.CompilerParams(vmem_limit_bytes=16 * 2**20),
        cost_estimate=pl.CostEstimate(flops=flops, bytes_accessed=moved, transcendentals=0),
    )(*args)


def shape(*dims, dtype=BF16):
    return jax.ShapeDtypeStruct(dims, dtype)


def shift_z(value, by):
    return lax.ppermute(value, "z", [(i, (i + by) % NZ) for i in range(NZ)])


def swap_cores(value):
    return lax.ppermute(value, "c", [(0, 1), (1, 0)])


def swap_y(value, k):
    return lax.ppermute(value, "yl", [(i, i ^ k) for i in range(NYL)])


def dot(a, b, dims):
    return lax.dot_general(a, b, (dims, ((), ())), preferred_element_type=F32)


def tie(*values):
    return lax.optimization_barrier(values)


def prepare_kernel(acts, upstream, send, turned):
    tokens, width = acts.shape
    keys = upstream.shape[1]
    rows = width // (NZ * NYL)
    stream = acts[...].astype(F32)
    radius = jnp.sqrt(jnp.mean(stream * stream, axis=1, keepdims=True) + norm_eps)
    for i in range(width // LANES):
        at = slice(i * LANES, (i + 1) * LANES)
        turned[at, :] = acts[:, at].astype(F32).T.astype(BF16)
    for j in range(NYL):
        for z in range(NZ):
            low = (z * NYL + j) * rows
            send[j, z * rows : (z + 1) * rows, :] = turned[low : low + rows, :]
    for i in range(keys // LANES):
        at = slice(i * LANES, (i + 1) * LANES)
        shared = (upstream[:, at].astype(F32) / radius).T.astype(BF16)
        low = NZ * rows + i * LANES
        for j in range(NYL):
            send[j, low : low + LANES, :] = shared


def gradient_kernel(scale, got, gains, keep, give, tile, shared, held):
    tokens = got.shape[2]
    width = gains.shape[0]
    rows = width // NZ
    for t in range(NYL):
        at = slice(t * tokens, (t + 1) * tokens)
        tile[:, at] = got[t, :width, :]
        shared[:, at] = got[t, width:, :]
    up = shared[...]
    for z in range(NZ):
        at = slice(z * rows, (z + 1) * rows)
        held[at, :] = (dot(tile[at, :], up, ((1,), (1,))) * (gains[at, :] * scale)).astype(BF16)
    j = lax.axis_index("yl")
    mine = lax.axis_index("z")
    for k in range(NZ):
        out = give if k % 2 else keep
        to = k - k % 2 + lax.rem(mine + k, 2)
        for i in range(rows // GROUP):
            z = lax.rem(lax.div(7 * j + i, 4) - to + NZ, NZ)
            out[k // 2, i] = held[pl.ds(pl.multiple_of(z * rows + i * GROUP, GROUP), GROUP), :]


def load_shared(got, width, shared):
    tokens = got.shape[2]
    for t in range(NYL):
        shared[:, t * tokens : (t + 1) * tokens] = got[t, width:, :]
    return shared[...]


def stats_kernel(got, weights, gains, stats, shared):
    tokens = got.shape[2]
    width = weights.shape[0]
    rows = width // NZ
    up = load_shared(got, width, shared)
    cross = [jnp.zeros((1, tokens), F32) for _ in range(NYL)]
    square = [jnp.zeros((1, tokens), F32) for _ in range(NYL)]
    for z in range(NZ):
        at = slice(z * rows, (z + 1) * rows)
        value = dot(weights[at, :], up, ((1,), (0,))) * gains[at, :]
        for t in range(NYL):
            wide = got[t, at, :].astype(F32)
            cross[t] = cross[t] + jnp.sum(value[:, t * tokens : (t + 1) * tokens] * wide, axis=0, keepdims=True)
            square[t] = square[t] + jnp.sum(wide * wide, axis=0, keepdims=True)
    for t in range(NYL):
        to = slice(t * tokens, (t + 1) * tokens)
        for copy in range(NYL):
            stats[copy, 0:1, to] = cross[t]
            stats[copy, 1:2, to] = square[t]


def branch_kernel(full, got, weights, gains, stats, out, shared):
    total = stats[0]
    for k in range(1, NYL):
        total = total + stats[k]
    pull = total[0:1, :] / full / (total[1:2, :] / full + norm_eps)
    tokens = got.shape[2]
    rows = out.shape[1]
    up = load_shared(got, weights.shape[0], shared)
    for i in range(NPAIR):
        at = slice(i * rows, (i + 1) * rows)
        value = dot(weights[at, :], up, ((1,), (0,))) * gains[at, :]
        for t in range(NYL):
            to = slice(t * tokens, (t + 1) * tokens)
            out[i, :, to] = (value[:, to] - got[t, at, :].astype(F32) * pull[:, to]).astype(BF16)


def suffix_kernel(spread, out):
    last = (lax.axis_index("c") == 1).astype(F32)
    run = jnp.zeros(spread.shape[1:], F32)
    for pair in range(NPAIR - 1, -1, -1):
        value = spread[pair].astype(F32)
        out[pair] = (run + value * last).astype(BF16)
        run = run + value


def section_kernel(spread, got, out):
    run = jnp.zeros(spread.shape[1:], F32)
    for pair in range(NPAIR - 1, -1, -1):
        run = run + spread[pair].astype(F32)
        value = run + got[pair].astype(F32)
        for t in range(NYL):
            out[pair * NYL + t] = value[:, t * LANES : (t + 1) * LANES].astype(BF16)


def final_kernel(turned, out):
    for i in range(out.shape[1] // LANES):
        at = slice(i * LANES, (i + 1) * LANES)
        out[:, at] = turned[at, :].astype(F32).T.astype(BF16)


def add_kernel(keep, got, *outs):
    h = lax.div(lax.axis_index("z"), 2)
    for k, out in enumerate(outs):
        at = lax.rem(h + k, NZ // 2)
        out[...] = (keep[at].astype(F32) + got[at].astype(F32)).astype(BF16)


def sum_kernel(*refs):
    *terms, out = refs
    total = terms[0][...].astype(F32)
    for term in terms[1:]:
        total = total + term[...].astype(F32)
    out[...] = total.astype(BF16)


def route_kernel(owners, *refs):
    parts, (keep, give, stage) = refs[:NYL], refs[NYL:]
    for k, part in enumerate(parts):
        stage[k] = part[...]
    z = lax.axis_index("z")
    j = lax.axis_index("yl")
    per = parts[0].shape[0]
    for i in range(NZ):
        out = give if i % 2 else keep
        out[i // 2] = jnp.zeros(out.shape[1:], BF16)
        place = (i - i % 2 + lax.rem(z + i, 2)) * NYL + j
        for b in range(owners.shape[1]):

            @pl.when(owners[0, b] == place)
            def _():
                for q in range(NYL):
                    group = 32 * b + NYL * z + q
                    shard = lax.div(group, per)
                    which = lax.rem(shard, NYL) ^ j
                    out[i // 2, q * GROUP : (q + 1) * GROUP, :] = stage[which, group - shard * per]


def pair_kernel(keep, got, *outs):
    h = lax.div(lax.axis_index("z"), 2)
    for k, out in enumerate(outs):
        at = lax.rem(h + k, NZ // 2)
        out[0] = keep[at]
        out[1] = got[at]


def shampoo_kernel(*refs):
    *parts, left, right, left_gram, right_gram, precond, grads = refs
    z = lax.axis_index("z")
    rows = parts[0].shape[1]
    for k, part in enumerate(parts):
        source = lax.rem(z + NZ - 2 * k, NZ)
        grads[pl.ds(pl.multiple_of(source * rows, rows), rows), :] = part[0]
        grads[pl.ds(pl.multiple_of((source ^ 1) * rows, rows), rows), :] = part[1]
    block = grads[...]
    middle = dot(left[...], block, ((1,), (0,))).astype(BF16)
    precond[...] = dot(middle, right[...], ((1,), (0,))).astype(BF16)
    left_gram[...] = (dot(block, block, ((1,), (1,))) / block.shape[0]).astype(BF16)
    right_gram[...] = (dot(block, block, ((0,), (0,))) / block.shape[0]).astype(BF16)


def body(acts, norm_gain, proj, out_grad, owner_slot, left_root, right_root):
    acts, gain, upstream, shard = acts[0], norm_gain[0], out_grad[0], proj[0]
    tokens, width = acts.shape
    rows, keys = shard.shape
    side = left_root.shape[-1]
    quarter = width // NYL
    line = NYL * tokens
    per = rows // GROUP

    (send,) = call(
        prepare_kernel,
        [shape(NYL, quarter + keys, tokens)],
        [acts, upstream],
        scratch=[pltpu.VMEM((width, tokens), BF16)],
    )
    got = lax.all_to_all(send, "yl", 0, 0)
    gains = lax.dynamic_index_in_dim(gain.reshape(NZ, NYL, rows), lax.axis_index("yl"), 1, False)
    gains = gains.reshape(quarter, 1)
    weights = lax.all_gather(shard, "z", axis=0, tiled=True)
    got, weights, gains = tie(got, weights, gains)
    scale = (tokens * NZ * NYL) ** (-0.5)
    chunk = shape(NZ // 2, per, GROUP, keys)
    chunks, away = call(
        lambda *refs: gradient_kernel(scale, *refs),
        [chunk, chunk],
        [got, gains],
        scratch=[pltpu.VMEM((quarter, line), BF16), pltpu.VMEM((keys, line), BF16), pltpu.VMEM((quarter, keys), BF16)],
        flops=2 * quarter * line * keys,
    )

    near = lax.ppermute(away, "z", [(i, i ^ 1) for i in range(NZ)])
    got, away = tie(got, away)
    (stats,) = call(
        stats_kernel,
        [shape(NYL, 2, line, dtype=F32)],
        [got, weights, gains],
        scratch=[pltpu.VMEM((keys, line), BF16)],
        flops=2 * quarter * line * keys,
    )
    stats = lax.all_to_all(stats, "yl", 0, 0)
    (branch,) = call(
        lambda *refs: branch_kernel(width, *refs),
        [shape(NPAIR, quarter // NPAIR, line)],
        [got, weights, gains, stats],
        scratch=[pltpu.VMEM((keys, line), BF16)],
        flops=2 * quarter * line * keys,
    )
    branch, near = tie(branch, near)

    spread = lax.all_to_all(branch, PAIRS, 0, 0)
    terms = call(add_kernel, [shape(per, GROUP, keys)] * (NZ // 2), [chunks, near])
    terms = [terms[0]] + [shift_z(terms[k], 2 * k) for k in range(1, NZ // 2)]
    (grads,) = call(sum_kernel, [shape(per, GROUP, keys)], terms)
    spread, grads = tie(spread, grads)
    (give,) = call(suffix_kernel, [shape(NPAIR, quarter // NPAIR, line)], [spread])
    take = swap_cores(give)
    parts = [grads] + [swap_y(grads, k) for k in range(1, NYL)]
    (sums,) = call(section_kernel, [shape(NPAIR * NYL, quarter // NPAIR, tokens)], [spread, take])
    sums, *parts = tie(sums, *parts)
    home = lax.all_to_all(sums, (*PAIRS, "yl"), 0, 0).reshape(width, tokens)

    half = shape(NZ // 2, side // NZ, keys)
    keep, away = call(
        route_kernel,
        [half, half],
        [owner_slot, *parts],
        scratch=[pltpu.VMEM((NYL, per, GROUP, keys), BF16)],
        smem=(0,),
    )
    near = lax.ppermute(away, "z", [(i, i ^ 1) for i in range(NZ)])
    parts = call(pair_kernel, [shape(2, side // NZ, keys)] * (NZ // 2), [keep, near])
    parts = [parts[0]] + [shift_z(parts[k], 2 * k) for k in range(1, NZ // 2)]
    out = shape(side, side)
    left_gram, right_gram, precond = call(
        shampoo_kernel,
        [out, out, out],
        [*parts, left_root[0, 0], right_root[0, 0]],
        scratch=[pltpu.VMEM((side, side), BF16)],
        flops=8 * side**3,
    )
    home, left_gram, right_gram, precond = tie(home, left_gram, right_gram, precond)
    (section_grad,) = call(final_kernel, [shape(tokens, width)], [home])
    return section_grad[None], left_gram[None, None], right_gram[None, None], precond[None, None]


def solution(mesh):
    split = Mesh(mesh.devices.reshape(NX, NYH, NC, NZ, NYL), (*SEC, *DP))
    in_specs = (
        P(SEC, DP, None),
        P(SEC, None),
        P(SEC, DP, None),
        P(SEC, DP, None),
        P(SEC, None),
        P(SEC, DP, None, None),
        P(SEC, DP, None, None),
    )
    out_specs = (
        P(SEC, DP, None),
        P(SEC, DP, None, None),
        P(SEC, DP, None, None),
        P(SEC, DP, None, None),
    )
    return jax.shard_map(body, mesh=split, in_specs=in_specs, out_specs=out_specs, check_vma=False)
```

```python
import jax
import jax.numpy as jnp
from jax import lax
from jax.experimental import pallas as pl
from jax.experimental.pallas import tpu as pltpu
from jax.sharding import Mesh, PartitionSpec as P

norm_eps = 1e-06
SEC = ("x", "yh", "c")
DP = ("z", "yl")
NX, NYH, NC, NZ, NYL = 4, 2, 2, 8, 4
PAIRS = ("x", "yh")
NPAIR = NX * NYH
LANES = 128
GROUP = 16
BF16, F32 = jnp.bfloat16, jnp.float32


def call(kernel, outs, args, scratch=(), flops=0, smem=()):
    specs = [pl.BlockSpec(memory_space=pltpu.SMEM if i in smem else pltpu.VMEM) for i in range(len(args))]
    moved = sum(a.size * a.dtype.itemsize for a in (*args, *outs))
    return pl.pallas_call(
        kernel,
        out_shape=outs,
        in_specs=specs,
        out_specs=[pl.BlockSpec(memory_space=pltpu.VMEM) for _ in outs],
        scratch_shapes=list(scratch),
        compiler_params=pltpu.CompilerParams(vmem_limit_bytes=16 * 2**20),
        cost_estimate=pl.CostEstimate(flops=flops, bytes_accessed=moved, transcendentals=0),
    )(*args)


def shape(*dims, dtype=BF16):
    return jax.ShapeDtypeStruct(dims, dtype)


def shift_z(value, by):
    return lax.ppermute(value, "z", [(i, (i + by) % NZ) for i in range(NZ)])


def swap_cores(value):
    return lax.ppermute(value, "c", [(0, 1), (1, 0)])


def swap_y(value, k):
    return lax.ppermute(value, "yl", [(i, i ^ k) for i in range(NYL)])


def dot(a, b, dims):
    return lax.dot_general(a, b, (dims, ((), ())), preferred_element_type=F32)


def tie(*values):
    return lax.optimization_barrier(values)


def prepare_kernel(acts, upstream, send, turned):
    tokens, width = acts.shape
    keys = upstream.shape[1]
    rows = width // (NZ * NYL)
    stream = acts[...].astype(F32)
    radius = jnp.sqrt(jnp.mean(stream * stream, axis=1, keepdims=True) + norm_eps)
    for i in range(width // LANES):
        at = slice(i * LANES, (i + 1) * LANES)
        turned[at, :] = acts[:, at].astype(F32).T.astype(BF16)
    for j in range(NYL):
        for z in range(NZ):
            low = (z * NYL + j) * rows
            send[j, z * rows : (z + 1) * rows, :] = turned[low : low + rows, :]
    for i in range(keys // LANES):
        at = slice(i * LANES, (i + 1) * LANES)
        shared = (upstream[:, at].astype(F32) / radius).T.astype(BF16)
        low = NZ * rows + i * LANES
        for j in range(NYL):
            send[j, low : low + LANES, :] = shared


def gradient_kernel(scale, got, gains, keep, give, tile, shared, held):
    tokens = got.shape[2]
    width = gains.shape[0]
    rows = width // NZ
    for t in range(NYL):
        at = slice(t * tokens, (t + 1) * tokens)
        tile[:, at] = got[t, :width, :]
        shared[:, at] = got[t, width:, :]
    up = shared[...]
    for z in range(NZ):
        at = slice(z * rows, (z + 1) * rows)
        held[at, :] = (dot(tile[at, :], up, ((1,), (1,))) * (gains[at, :] * scale)).astype(BF16)
    j = lax.axis_index("yl")
    mine = lax.axis_index("z")
    for k in range(NZ):
        out = give if k % 2 else keep
        to = k - k % 2 + lax.rem(mine + k, 2)
        for i in range(rows // GROUP):
            z = lax.rem(lax.div(7 * j + i, 4) - to + NZ, NZ)
            out[k // 2, i] = held[pl.ds(pl.multiple_of(z * rows + i * GROUP, GROUP), GROUP), :]


def load_shared(got, width, shared):
    tokens = got.shape[2]
    for t in range(NYL):
        shared[:, t * tokens : (t + 1) * tokens] = got[t, width:, :]
    return shared[...]


def stats_kernel(got, weights, gains, stats, shared):
    tokens = got.shape[2]
    width = weights.shape[0]
    rows = width // NZ
    up = load_shared(got, width, shared)
    cross = [jnp.zeros((1, tokens), F32) for _ in range(NYL)]
    square = [jnp.zeros((1, tokens), F32) for _ in range(NYL)]
    for z in range(NZ):
        at = slice(z * rows, (z + 1) * rows)
        value = dot(weights[at, :], up, ((1,), (0,))) * gains[at, :]
        for t in range(NYL):
            wide = got[t, at, :].astype(F32)
            cross[t] = cross[t] + jnp.sum(value[:, t * tokens : (t + 1) * tokens] * wide, axis=0, keepdims=True)
            square[t] = square[t] + jnp.sum(wide * wide, axis=0, keepdims=True)
    for t in range(NYL):
        to = slice(t * tokens, (t + 1) * tokens)
        for copy in range(NYL):
            stats[copy, 0:1, to] = cross[t]
            stats[copy, 1:2, to] = square[t]


def branch_kernel(full, got, weights, gains, stats, out, shared):
    total = stats[0]
    for k in range(1, NYL):
        total = total + stats[k]
    pull = total[0:1, :] / full / (total[1:2, :] / full + norm_eps)
    tokens = got.shape[2]
    rows = out.shape[1]
    up = load_shared(got, weights.shape[0], shared)
    for i in range(NPAIR):
        at = slice(i * rows, (i + 1) * rows)
        value = dot(weights[at, :], up, ((1,), (0,))) * gains[at, :]
        for t in range(NYL):
            to = slice(t * tokens, (t + 1) * tokens)
            out[i, :, to] = (value[:, to] - got[t, at, :].astype(F32) * pull[:, to]).astype(BF16)


def suffix_kernel(spread, out):
    last = (lax.axis_index("c") == 1).astype(F32)
    run = jnp.zeros(spread.shape[1:], F32)
    for pair in range(NPAIR - 1, -1, -1):
        value = spread[pair].astype(F32)
        out[pair] = (run + value * last).astype(BF16)
        run = run + value


def section_kernel(spread, got, out):
    run = jnp.zeros(spread.shape[1:], F32)
    for pair in range(NPAIR - 1, -1, -1):
        run = run + spread[pair].astype(F32)
        value = run + got[pair].astype(F32)
        for t in range(NYL):
            out[pair * NYL + t] = value[:, t * LANES : (t + 1) * LANES].astype(BF16)


def final_kernel(turned, out):
    for i in range(out.shape[1] // LANES):
        at = slice(i * LANES, (i + 1) * LANES)
        out[:, at] = turned[at, :].astype(F32).T.astype(BF16)


def add_kernel(keep, got, *outs):
    h = lax.div(lax.axis_index("z"), 2)
    for k, out in enumerate(outs):
        at = lax.rem(h + k, NZ // 2)
        out[...] = (keep[at].astype(F32) + got[at].astype(F32)).astype(BF16)


def sum_kernel(*refs):
    *terms, out = refs
    total = terms[0][...].astype(F32)
    for term in terms[1:]:
        total = total + term[...].astype(F32)
    out[...] = total.astype(BF16)


def route_kernel(owners, *refs):
    parts, (keep, give, stage) = refs[:NYL], refs[NYL:]
    for k, part in enumerate(parts):
        stage[k] = part[...]
    z = lax.axis_index("z")
    j = lax.axis_index("yl")
    per = parts[0].shape[0]
    for i in range(NZ):
        out = give if i % 2 else keep
        out[i // 2] = jnp.zeros(out.shape[1:], BF16)
        place = (i - i % 2 + lax.rem(z + i, 2)) * NYL + j
        for b in range(owners.shape[1]):

            @pl.when(owners[0, b] == place)
            def _():
                for q in range(NYL):
                    group = 32 * b + NYL * z + q
                    shard = lax.div(group, per)
                    which = lax.rem(shard, NYL) ^ j
                    out[i // 2, q * GROUP : (q + 1) * GROUP, :] = stage[which, group - shard * per]


def pair_kernel(keep, got, *outs):
    h = lax.div(lax.axis_index("z"), 2)
    for k, out in enumerate(outs):
        at = lax.rem(h + k, NZ // 2)
        out[0] = keep[at]
        out[1] = got[at]


def shampoo_kernel(*refs):
    *parts, left, right, left_gram, right_gram, precond, grads = refs
    z = lax.axis_index("z")
    rows = parts[0].shape[1]
    for k, part in enumerate(parts):
        source = lax.rem(z + NZ - 2 * k, NZ)
        grads[pl.ds(pl.multiple_of(source * rows, rows), rows), :] = part[0]
        grads[pl.ds(pl.multiple_of((source ^ 1) * rows, rows), rows), :] = part[1]
    block = grads[...]
    middle = dot(left[...], block, ((1,), (0,))).astype(BF16)
    precond[...] = dot(middle, right[...], ((1,), (0,))).astype(BF16)
    left_gram[...] = (dot(block, block, ((1,), (1,))) / block.shape[0]).astype(BF16)
    right_gram[...] = (dot(block, block, ((0,), (0,))) / block.shape[0]).astype(BF16)


def body(acts, norm_gain, proj, out_grad, owner_slot, left_root, right_root):
    acts, gain, upstream, shard = acts[0], norm_gain[0], out_grad[0], proj[0]
    tokens, width = acts.shape
    rows, keys = shard.shape
    side = left_root.shape[-1]
    quarter = width // NYL
    line = NYL * tokens
    per = rows // GROUP

    (send,) = call(
        prepare_kernel,
        [shape(NYL, quarter + keys, tokens)],
        [acts, upstream],
        scratch=[pltpu.VMEM((width, tokens), BF16)],
    )
    got = lax.all_to_all(send, "yl", 0, 0)
    gains = lax.dynamic_index_in_dim(gain.reshape(NZ, NYL, rows), lax.axis_index("yl"), 1, False)
    gains = gains.reshape(quarter, 1)
    weights = lax.all_gather(shard, "z", axis=0, tiled=True)
    got, weights, gains = tie(got, weights, gains)
    scale = (tokens * NZ * NYL) ** (-0.5)
    chunk = shape(NZ // 2, per, GROUP, keys)
    chunks, away = call(
        lambda *refs: gradient_kernel(scale, *refs),
        [chunk, chunk],
        [got, gains],
        scratch=[pltpu.VMEM((quarter, line), BF16), pltpu.VMEM((keys, line), BF16), pltpu.VMEM((quarter, keys), BF16)],
        flops=2 * quarter * line * keys,
    )

    near = lax.ppermute(away, "z", [(i, i ^ 1) for i in range(NZ)])
    got, away = tie(got, away)
    (stats,) = call(
        stats_kernel,
        [shape(NYL, 2, line, dtype=F32)],
        [got, weights, gains],
        scratch=[pltpu.VMEM((keys, line), BF16)],
        flops=2 * quarter * line * keys,
    )
    stats = lax.all_to_all(stats, "yl", 0, 0)
    (branch,) = call(
        lambda *refs: branch_kernel(width, *refs),
        [shape(NPAIR, quarter // NPAIR, line)],
        [got, weights, gains, stats],
        scratch=[pltpu.VMEM((keys, line), BF16)],
        flops=2 * quarter * line * keys,
    )
    branch, near = tie(branch, near)

    spread = lax.all_to_all(branch, PAIRS, 0, 0)
    terms = call(add_kernel, [shape(per, GROUP, keys)] * (NZ // 2), [chunks, near])
    terms = [terms[0]] + [shift_z(terms[k], 2 * k) for k in range(1, NZ // 2)]
    (grads,) = call(sum_kernel, [shape(per, GROUP, keys)], terms)
    spread, grads = tie(spread, grads)
    (give,) = call(suffix_kernel, [shape(NPAIR, quarter // NPAIR, line)], [spread])
    take = swap_cores(give)
    parts = [grads] + [swap_y(grads, k) for k in range(1, NYL)]
    (sums,) = call(section_kernel, [shape(NPAIR * NYL, quarter // NPAIR, tokens)], [spread, take])
    sums, *parts = tie(sums, *parts)
    home = lax.all_to_all(sums, (*PAIRS, "yl"), 0, 0).reshape(width, tokens)

    half = shape(NZ // 2, side // NZ, keys)
    keep, away = call(
        route_kernel,
        [half, half],
        [owner_slot, *parts],
        scratch=[pltpu.VMEM((NYL, per, GROUP, keys), BF16)],
        smem=(0,),
    )
    near = lax.ppermute(away, "z", [(i, i ^ 1) for i in range(NZ)])
    parts = call(pair_kernel, [shape(2, side // NZ, keys)] * (NZ // 2), [keep, near])
    parts = [parts[0]] + [shift_z(parts[k], 2 * k) for k in range(1, NZ // 2)]
    (section_grad,) = call(final_kernel, [shape(tokens, width)], [home])
    section_grad, *parts = tie(section_grad, *parts)
    out = shape(side, side)
    left_gram, right_gram, precond = call(
        shampoo_kernel,
        [out, out, out],
        [*parts, left_root[0, 0], right_root[0, 0]],
        scratch=[pltpu.VMEM((side, side), BF16)],
        flops=8 * side**3,
    )
    return section_grad[None], left_gram[None, None], right_gram[None, None], precond[None, None]


def solution(mesh):
    split = Mesh(mesh.devices.reshape(NX, NYH, NC, NZ, NYL), (*SEC, *DP))
    in_specs = (
        P(SEC, DP, None),
        P(SEC, None),
        P(SEC, DP, None),
        P(SEC, DP, None),
        P(SEC, None),
        P(SEC, DP, None, None),
        P(SEC, DP, None, None),
    )
    out_specs = (
        P(SEC, DP, None),
        P(SEC, DP, None, None),
        P(SEC, DP, None, None),
        P(SEC, DP, None, None),
    )
    return jax.shard_map(body, mesh=split, in_specs=in_specs, out_specs=out_specs, check_vma=False)
```

```python
import jax
import jax.numpy as jnp
from jax import lax
from jax.experimental import pallas as pl
from jax.experimental.pallas import tpu as pltpu
from jax.sharding import Mesh, PartitionSpec as P

norm_eps = 1e-06
SEC = ("x", "yh", "c")
DP = ("z", "yl")
NX, NYH, NC, NZ, NYL = 4, 2, 2, 8, 4
PAIRS = ("x", "yh")
NPAIR = NX * NYH
LANES = 128
GROUP = 16
BF16, F32 = jnp.bfloat16, jnp.float32


def call(kernel, outs, args, scratch=(), flops=0, smem=()):
    specs = [pl.BlockSpec(memory_space=pltpu.SMEM if i in smem else pltpu.VMEM) for i in range(len(args))]
    moved = sum(a.size * a.dtype.itemsize for a in (*args, *outs))
    return pl.pallas_call(
        kernel,
        out_shape=outs,
        in_specs=specs,
        out_specs=[pl.BlockSpec(memory_space=pltpu.VMEM) for _ in outs],
        scratch_shapes=list(scratch),
        compiler_params=pltpu.CompilerParams(vmem_limit_bytes=16 * 2**20),
        cost_estimate=pl.CostEstimate(flops=flops, bytes_accessed=moved, transcendentals=0),
    )(*args)


def shape(*dims, dtype=BF16):
    return jax.ShapeDtypeStruct(dims, dtype)


def shift_z(value, by):
    return lax.ppermute(value, "z", [(i, (i + by) % NZ) for i in range(NZ)])


def swap_cores(value):
    return lax.ppermute(value, "c", [(0, 1), (1, 0)])


def swap_y(value, k):
    return lax.ppermute(value, "yl", [(i, i ^ k) for i in range(NYL)])


def dot(a, b, dims):
    return lax.dot_general(a, b, (dims, ((), ())), preferred_element_type=F32)


def tie(*values):
    return lax.optimization_barrier(values)


def prepare_kernel(acts, upstream, send, turned):
    tokens, width = acts.shape
    keys = upstream.shape[1]
    rows = width // (NZ * NYL)
    stream = acts[...].astype(F32)
    radius = jnp.sqrt(jnp.mean(stream * stream, axis=1, keepdims=True) + norm_eps)
    for i in range(width // LANES):
        at = slice(i * LANES, (i + 1) * LANES)
        turned[at, :] = acts[:, at].astype(F32).T.astype(BF16)
    for j in range(NYL):
        for z in range(NZ):
            low = (z * NYL + j) * rows
            send[j, z * rows : (z + 1) * rows, :] = turned[low : low + rows, :]
    for i in range(keys // LANES):
        at = slice(i * LANES, (i + 1) * LANES)
        shared = (upstream[:, at].astype(F32) / radius).T.astype(BF16)
        low = NZ * rows + i * LANES
        for j in range(NYL):
            send[j, low : low + LANES, :] = shared


def gradient_kernel(scale, other, got, gains, out, tile, column, shared):
    tokens = got.shape[2]
    width = gains.shape[0]
    rows = width // NZ
    up = load_shared(got, width, shared)
    j = lax.axis_index("yl")
    parity = lax.rem(lax.axis_index("z") + other, 2)
    for k in range(NZ // 2):
        for i in range(rows // GROUP):
            z = lax.rem(lax.div(7 * j + i, 4) - 2 * k - parity + NZ, NZ)
            at = pl.ds(pl.multiple_of(z * rows + i * GROUP, GROUP), GROUP)
            to = slice(k * rows + i * GROUP, k * rows + (i + 1) * GROUP)
            for t in range(NYL):
                tile[to, t * tokens : (t + 1) * tokens] = got[t, at, :]
            column[to, :] = gains[at, :]
    for k in range(NZ // 2):
        at = slice(k * rows, (k + 1) * rows)
        value = (dot(tile[at, :], up, ((1,), (1,))) * (column[at, :] * scale)).astype(BF16)
        for i in range(rows // GROUP):
            out[k, i] = value[i * GROUP : (i + 1) * GROUP, :]


def load_shared(got, width, shared):
    tokens = got.shape[2]
    for t in range(NYL):
        shared[:, t * tokens : (t + 1) * tokens] = got[t, width:, :]
    return shared[...]


def stats_kernel(got, weights, gains, stats, shared):
    tokens = got.shape[2]
    width = weights.shape[0]
    rows = width // NZ
    up = load_shared(got, width, shared)
    cross = [jnp.zeros((1, tokens), F32) for _ in range(NYL)]
    square = [jnp.zeros((1, tokens), F32) for _ in range(NYL)]
    for z in range(NZ):
        at = slice(z * rows, (z + 1) * rows)
        value = dot(weights[at, :], up, ((1,), (0,))) * gains[at, :]
        for t in range(NYL):
            wide = got[t, at, :].astype(F32)
            cross[t] = cross[t] + jnp.sum(value[:, t * tokens : (t + 1) * tokens] * wide, axis=0, keepdims=True)
            square[t] = square[t] + jnp.sum(wide * wide, axis=0, keepdims=True)
    for t in range(NYL):
        to = slice(t * tokens, (t + 1) * tokens)
        for copy in range(NYL):
            stats[copy, 0:1, to] = cross[t]
            stats[copy, 1:2, to] = square[t]


def branch_kernel(full, got, weights, gains, stats, out, shared):
    total = stats[0]
    for k in range(1, NYL):
        total = total + stats[k]
    pull = total[0:1, :] / full / (total[1:2, :] / full + norm_eps)
    tokens = got.shape[2]
    rows = out.shape[1]
    up = load_shared(got, weights.shape[0], shared)
    for i in range(NPAIR):
        at = slice(i * rows, (i + 1) * rows)
        value = dot(weights[at, :], up, ((1,), (0,))) * gains[at, :]
        for t in range(NYL):
            to = slice(t * tokens, (t + 1) * tokens)
            out[i, :, to] = (value[:, to] - got[t, at, :].astype(F32) * pull[:, to]).astype(BF16)


def suffix_kernel(spread, out):
    last = (lax.axis_index("c") == 1).astype(F32)
    run = jnp.zeros(spread.shape[1:], F32)
    for pair in range(NPAIR - 1, -1, -1):
        value = spread[pair].astype(F32)
        out[pair] = (run + value * last).astype(BF16)
        run = run + value


def section_kernel(spread, got, out):
    run = jnp.zeros(spread.shape[1:], F32)
    for pair in range(NPAIR - 1, -1, -1):
        run = run + spread[pair].astype(F32)
        value = run + got[pair].astype(F32)
        for t in range(NYL):
            out[pair * NYL + t] = value[:, t * LANES : (t + 1) * LANES].astype(BF16)


def final_kernel(turned, out):
    for i in range(out.shape[1] // LANES):
        at = slice(i * LANES, (i + 1) * LANES)
        out[:, at] = turned[at, :].astype(F32).T.astype(BF16)


def add_kernel(keep, got, *outs):
    h = lax.div(lax.axis_index("z"), 2)
    for k, out in enumerate(outs):
        at = lax.rem(h + k, NZ // 2)
        out[...] = (keep[at].astype(F32) + got[at].astype(F32)).astype(BF16)


def sum_kernel(*refs):
    *terms, out = refs
    total = terms[0][...].astype(F32)
    for term in terms[1:]:
        total = total + term[...].astype(F32)
    out[...] = total.astype(BF16)


def route_kernel(owners, *refs):
    parts, (keep, give, stage) = refs[:NYL], refs[NYL:]
    for k, part in enumerate(parts):
        stage[k] = part[...]
    z = lax.axis_index("z")
    j = lax.axis_index("yl")
    per = parts[0].shape[0]
    for i in range(NZ):
        out = give if i % 2 else keep
        out[i // 2] = jnp.zeros(out.shape[1:], BF16)
        place = (i - i % 2 + lax.rem(z + i, 2)) * NYL + j
        for b in range(owners.shape[1]):

            @pl.when(owners[0, b] == place)
            def _():
                for q in range(NYL):
                    group = 32 * b + NYL * z + q
                    shard = lax.div(group, per)
                    which = lax.rem(shard, NYL) ^ j
                    out[i // 2, q * GROUP : (q + 1) * GROUP, :] = stage[which, group - shard * per]


def pair_kernel(keep, got, *outs):
    h = lax.div(lax.axis_index("z"), 2)
    for k, out in enumerate(outs):
        at = lax.rem(h + k, NZ // 2)
        out[0] = keep[at]
        out[1] = got[at]


def shampoo_kernel(*refs):
    *parts, left, right, left_gram, right_gram, precond, grads = refs
    z = lax.axis_index("z")
    rows = parts[0].shape[1]
    for k, part in enumerate(parts):
        source = lax.rem(z + NZ - 2 * k, NZ)
        grads[pl.ds(pl.multiple_of(source * rows, rows), rows), :] = part[0]
        grads[pl.ds(pl.multiple_of((source ^ 1) * rows, rows), rows), :] = part[1]
    block = grads[...]
    middle = dot(left[...], block, ((1,), (0,))).astype(BF16)
    precond[...] = dot(middle, right[...], ((1,), (0,))).astype(BF16)
    left_gram[...] = (dot(block, block, ((1,), (1,))) / block.shape[0]).astype(BF16)
    right_gram[...] = (dot(block, block, ((0,), (0,))) / block.shape[0]).astype(BF16)


def body(acts, norm_gain, proj, out_grad, owner_slot, left_root, right_root):
    acts, gain, upstream, shard = acts[0], norm_gain[0], out_grad[0], proj[0]
    tokens, width = acts.shape
    rows, keys = shard.shape
    side = left_root.shape[-1]
    quarter = width // NYL
    line = NYL * tokens
    per = rows // GROUP

    (send,) = call(
        prepare_kernel,
        [shape(NYL, quarter + keys, tokens)],
        [acts, upstream],
        scratch=[pltpu.VMEM((width, tokens), BF16)],
    )
    got = lax.all_to_all(send, "yl", 0, 0)
    gains = lax.dynamic_index_in_dim(gain.reshape(NZ, NYL, rows), lax.axis_index("yl"), 1, False)
    gains = gains.reshape(quarter, 1)
    weights = lax.all_gather(shard, "z", axis=0, tiled=True)
    got, weights, gains = tie(got, weights, gains)
    scale = (tokens * NZ * NYL) ** (-0.5)
    chunk = shape(NZ // 2, per, GROUP, keys)

    def gradient(other, got, gains):
        return call(
            lambda *refs: gradient_kernel(scale, other, *refs),
            [chunk],
            [got, gains],
            scratch=[
                pltpu.VMEM((quarter // 2, line), BF16),
                pltpu.VMEM((quarter // 2, 1), F32),
                pltpu.VMEM((keys, line), BF16),
            ],
            flops=quarter * line * keys,
        )[0]

    away = gradient(1, got, gains)

    near = lax.ppermute(away, "z", [(i, i ^ 1) for i in range(NZ)])
    got, away = tie(got, away)
    (stats,) = call(
        stats_kernel,
        [shape(NYL, 2, line, dtype=F32)],
        [got, weights, gains],
        scratch=[pltpu.VMEM((keys, line), BF16)],
        flops=2 * quarter * line * keys,
    )
    got, gains, stats = tie(got, gains, stats)
    stats = lax.all_to_all(stats, "yl", 0, 0)
    chunks = gradient(0, got, gains)
    stats, chunks = tie(stats, chunks)
    (branch,) = call(
        lambda *refs: branch_kernel(width, *refs),
        [shape(NPAIR, quarter // NPAIR, line)],
        [got, weights, gains, stats],
        scratch=[pltpu.VMEM((keys, line), BF16)],
        flops=2 * quarter * line * keys,
    )
    branch, near = tie(branch, near)

    spread = lax.all_to_all(branch, PAIRS, 0, 0)
    terms = call(add_kernel, [shape(per, GROUP, keys)] * (NZ // 2), [chunks, near])
    terms = [terms[0]] + [shift_z(terms[k], 2 * k) for k in range(1, NZ // 2)]
    (grads,) = call(sum_kernel, [shape(per, GROUP, keys)], terms)
    spread, grads = tie(spread, grads)
    (give,) = call(suffix_kernel, [shape(NPAIR, quarter // NPAIR, line)], [spread])
    take = swap_cores(give)
    parts = [grads] + [swap_y(grads, k) for k in range(1, NYL)]
    (sums,) = call(section_kernel, [shape(NPAIR * NYL, quarter // NPAIR, tokens)], [spread, take])
    sums, *parts = tie(sums, *parts)
    home = lax.all_to_all(sums, (*PAIRS, "yl"), 0, 0).reshape(width, tokens)

    half = shape(NZ // 2, side // NZ, keys)
    keep, away = call(
        route_kernel,
        [half, half],
        [owner_slot, *parts],
        scratch=[pltpu.VMEM((NYL, per, GROUP, keys), BF16)],
        smem=(0,),
    )
    near = lax.ppermute(away, "z", [(i, i ^ 1) for i in range(NZ)])
    parts = call(pair_kernel, [shape(2, side // NZ, keys)] * (NZ // 2), [keep, near])
    parts = [parts[0]] + [shift_z(parts[k], 2 * k) for k in range(1, NZ // 2)]
    (section_grad,) = call(final_kernel, [shape(tokens, width)], [home])
    section_grad, *parts = tie(section_grad, *parts)
    out = shape(side, side)
    left_gram, right_gram, precond = call(
        shampoo_kernel,
        [out, out, out],
        [*parts, left_root[0, 0], right_root[0, 0]],
        scratch=[pltpu.VMEM((side, side), BF16)],
        flops=8 * side**3,
    )
    return section_grad[None], left_gram[None, None], right_gram[None, None], precond[None, None]


def solution(mesh):
    split = Mesh(mesh.devices.reshape(NX, NYH, NC, NZ, NYL), (*SEC, *DP))
    in_specs = (
        P(SEC, DP, None),
        P(SEC, None),
        P(SEC, DP, None),
        P(SEC, DP, None),
        P(SEC, None),
        P(SEC, DP, None, None),
        P(SEC, DP, None, None),
    )
    out_specs = (
        P(SEC, DP, None),
        P(SEC, DP, None, None),
        P(SEC, DP, None, None),
        P(SEC, DP, None, None),
    )
    return jax.shard_map(body, mesh=split, in_specs=in_specs, out_specs=out_specs, check_vma=False)
```
